32 devices in a mesh: dp: 4 (over y, core), ep: 8 (over z, x).
Axes of the slice: x: 2, y: 2, z: 4, core: 2. Of those that a mesh axis runs over, the one named last changes fastest.
Arguments:
- tokens: bfloat16 [4096, 2048], P(('dp', 'ep')), may hold values from -6 to 6
- expert_ids: int32 [4096, 6], P(('dp', 'ep')), may hold values from 0 to 63, all different within a row; in each aligned block of 128 rows (0 to 127, 128 to 255, ...) at most 13 rows name the same one
- gate_scales: float32 [4096, 6], P(('dp', 'ep')), may hold values from 0.05 to 0.5
- expert_slot: int32 [64], replicated, may hold values from 0 to 63, each once
- gate_weight: bfloat16 [64, 2048, 1408], P('ep', 'dp'), may hold values from -0.125 to 0.125
- up_weight: bfloat16 [64, 2048, 1408], P('ep', 'dp'), may hold values from -0.125 to 0.125
- down_weight: bfloat16 [64, 1408, 2048], P('ep', None, 'dp'), may hold values from -0.15625 to 0.15625
Outputs:
- mixed: bfloat16 [4096, 2048], P(('dp', 'ep'))
The draws below stay inside these ranges and needn't reach their ends.
Inputs may be any that keep to these rules, and one draw needn't show every extreme that they name: `expert_ids`: among the 128 tokens of one device no expert is chosen by more than 13; the 6 experts of a token differ. `expert_slot`: each expert has exactly one slot.
All inputs are finite; a program needn't handle non-finite values.
Results may differ from the reference program's by a relative error of at most 0.0057.
Values may be sent and summed in bfloat16 or wider, within the bound.
A program may use at most 256 MiB of HBM per device.

```python
import math
import jax
import jax.numpy as jnp
import numpy as np
from jax import lax

D = 2048
FF = 1408
EXPERTS = 64
TOP = 6
TOK_DEV = 128
C = 13
TOKENS = 4096
N_DP = 4
N_EP = 8


def levels(key, dims, split, smallest, top_value):
    gain, own = 1.0, jax.random.fold_in(key, 6)
    for axis_at, shards_of in split:
        steps = jnp.exp(jax.random.uniform(jax.random.fold_in(own, axis_at), (shards_of,), jnp.float32, smallest / len(split), top_value / len(split)))
        gain = gain * jnp.repeat(steps, dims[axis_at] // shards_of).reshape([-1 if axis == axis_at else 1 for axis in range(len(dims))])
    return gain


def assign_block(own_key, own, number, rows, amount, top, limit, slope):
    ranking = jax.random.permutation(own_key, amount)
    packed, usual = portions_of(amount, rows * top, limit, slope, True), portions_of(amount, rows * top, limit, slope, False)
    places = jnp.arange(amount)

    def named(tallies, turn):
        used = int((tallies > 0).sum())
        fixed = max(1, used // 4)
        moved = fixed + (places - fixed + turn * (used - fixed)) % max(1, amount - fixed)
        return jnp.zeros((amount,), jnp.int32).at[ranking[jnp.where(places < fixed, places, moved)]].set(jnp.asarray(tallies, jnp.int32))

    tallies = jnp.where(number % 4 == 0, named(packed, number // 4), named(usual, number - number // 4 - 1))
    mixed = jax.random.permutation(jax.random.fold_in(own, 3), amount)
    donor, receiver = mixed[0:amount // 2 * 2:2], mixed[1:amount // 2 * 2:2]
    room = jnp.minimum(tallies[donor] - 1, limit - tallies[receiver]) // 2
    room = jnp.where((donor == ranking[0]) | (receiver == ranking[0]) | (tallies[receiver] == 0), 0, jnp.maximum(room, 0))
    moved = jax.random.randint(jax.random.fold_in(own, 4), (amount // 2,), 0, 1 << 20) % (room + 1)
    tallies = tallies.at[donor].add(-moved).at[receiver].add(moved)
    items = jnp.searchsorted(jnp.cumsum(tallies), jnp.arange(rows * top), side="right").astype(jnp.int32)
    listing = items.reshape(top, rows).T
    listing = listing[jax.random.permutation(jax.random.fold_in(own, 1), rows)]
    turn = jax.random.randint(jax.random.fold_in(own, 2), (rows, 1), 0, top)
    return jnp.take_along_axis(listing, (jnp.arange(top)[None, :] + turn) % top, axis=1)


def portions_of(number_of, total, reach, slope, full):
    weights = [(1 << 20) // math.isqrt(grade ** slope) + 1 for grade in range(1, number_of + 1)]
    largest = reach if full else min(reach, max(-(-total // number_of), total * weights[0] // sum(weights)))
    least = 1 if total - largest >= number_of - 1 else 0
    given, rest = [largest] + [least] * (number_of - 1), total - largest - least * (number_of - 1)
    while rest > 0:
        candidates = [i for i in range(1, number_of) if given[i] < largest] or [i for i in range(1, number_of) if given[i] < reach]
        whole, left = sum([weights[i] for i in candidates]), rest
        for i in candidates:
            addition = min(reach - given[i], max(1, left * weights[i] // whole), rest)
            given[i] = given[i] + addition
            rest = rest - addition
    return np.array(given)


def gaussian(own_key, dims, spread, bound, split=(), kind=jnp.bfloat16):
    loudness = levels(own_key, dims, split, -0.22, 0.18) if split else 1.0
    array = jax.random.normal(own_key, dims, jnp.float32) * spread * loudness
    return jnp.minimum(jnp.maximum(array, -bound), bound).astype(kind)


def setup_inputs(seed: int = 0) -> dict:
    key_list = jax.random.split(jax.random.key(seed), 8)
    tokens = gaussian(key_list[0], (TOKENS, D), 1.0, 6.0, ((0, 32),))
    expert_ids_keys = jax.random.split(jax.random.fold_in(key_list[1], 1), TOKENS // TOK_DEV)
    expert_ids_turns = jax.random.permutation(jax.random.fold_in(key_list[1], 3), TOKENS // TOK_DEV)
    expert_ids = jax.vmap(lambda own, number: assign_block(jax.random.fold_in(key_list[1], 2), own, number, TOK_DEV, EXPERTS, TOP, C, 1))(expert_ids_keys, expert_ids_turns).reshape((TOKENS, TOP))
    gate_scales = jnp.clip(jnp.exp(math.log(0.5) - 2.3025851 * jax.random.uniform(key_list[2], (TOKENS, TOP), jnp.float32) ** levels(key_list[2], (TOKENS, TOP), ((0, 32),), -0.2, 0.2)), 0.05, 0.5)
    expert_slot = jax.random.permutation(key_list[3], EXPERTS).astype(jnp.int32)
    gate_weight = gaussian(key_list[4], (EXPERTS, D, FF), D ** -0.5, 0.125, ((0, 8), (1, 4)))
    up_weight = gaussian(key_list[5], (EXPERTS, D, FF), D ** -0.5, 0.125, ((0, 8), (1, 4)))
    down_weight = gaussian(key_list[6], (EXPERTS, FF, D), FF ** -0.5, 0.15625, ((0, 8), (2, 4)))
    return dict(tokens=tokens, expert_ids=expert_ids, gate_scales=gate_scales, expert_slot=expert_slot, gate_weight=gate_weight, up_weight=up_weight, down_weight=down_weight)


def reference(tokens, expert_ids, gate_scales, expert_slot, gate_weight, up_weight, down_weight):
    total = TOKENS * TOP
    ids = expert_ids.reshape(-1).astype(jnp.int32)
    scales = gate_scales.reshape(-1).astype(jnp.float32)
    order = jnp.argsort(ids, stable=True).astype(jnp.int32)
    counts = jnp.sum((ids[:, None] == jnp.arange(EXPERTS, dtype=jnp.int32)[None, :]).astype(jnp.int32), 0)
    starts = (jnp.cumsum(counts) - counts).astype(jnp.int32)
    width = N_DP * N_EP * C
    offsets = jnp.arange(width, dtype=jnp.int32)

    def one_expert(mixed, expert):
        position = jnp.minimum(starts[expert] + offsets, total - 1).astype(jnp.int32)
        valid = offsets < counts[expert]
        chosen = order[position]
        rows = chosen // TOP
        picked = tokens[rows]
        slot = expert_slot[expert]
        gate = jnp.dot(picked, gate_weight[slot], preferred_element_type=jnp.float32)
        up = jnp.dot(picked, up_weight[slot], preferred_element_type=jnp.float32)
        hidden = (jax.nn.silu(gate) * up).astype(jnp.bfloat16)
        output = jnp.dot(hidden, down_weight[slot], preferred_element_type=jnp.float32).astype(jnp.bfloat16)
        weight = jnp.where(valid, scales[chosen], jnp.zeros_like(scales[chosen]))
        mixed = mixed.at[rows].add(weight[:, None] * output.astype(jnp.float32))
        return mixed, None

    start = jnp.zeros((TOKENS, D), jnp.float32)
    mixed, _ = lax.scan(one_expert, start, jnp.arange(EXPERTS, dtype=jnp.int32))
    return mixed.astype(jnp.bfloat16)
```

```python
import jax
import jax.numpy as jnp
from jax import lax
from jax.sharding import PartitionSpec as P

C = 13
GROUP = 8
CHUNKS = 4
F32 = jnp.float32
BF16 = jnp.bfloat16


def local(tokens, expert_ids, gate_scales, expert_slot, gate_weight, up_weight, down_weight):
    tok = tokens.shape[0]
    top = expert_ids.shape[1]
    experts = expert_slot.shape[0]
    exp_dev, part_d, ff = gate_weight.shape
    n_dp = lax.axis_size("dp")
    n_ep = lax.axis_size("ep")
    sources = n_dp * n_ep
    groups = sources // GROUP
    inner = groups // 4
    span = GROUP * tok
    rows = GROUP * C
    me_dp = lax.axis_index("dp")
    me_ep = lax.axis_index("ep")
    core, far = me_dp % 2, me_dp // 2
    over_core = [(i, i ^ 1) for i in range(4)]
    over_far = [(i, i ^ 2) for i in range(4)]

    def relative(a):
        a = a.reshape((2, 2) + a.shape[1:])
        a = jnp.where(core == 0, a, jnp.concatenate([a[:, 1:], a[:, :1]], 1))
        return jnp.where(far == 0, a, jnp.concatenate([a[1:], a[:1]], 0))

    mine = lax.all_to_all(tokens, "dp", split_axis=1, concat_axis=0, tiled=True)
    every = lax.all_gather(mine, "ep", axis=0, tiled=True)
    every = every.reshape(4, inner, span, part_d)

    same = expert_ids[:, :, None] == jnp.arange(experts, dtype=jnp.int32)
    slot = jnp.sum(jnp.where(same, expert_slot, 0), 2)
    meta = jnp.concatenate([gate_scales, slot.astype(F32)], 1).T
    meta = lax.all_gather(meta, ("ep", "dp"), axis=0)
    here = meta[:, top:].astype(jnp.int32) - me_ep * exp_dev
    hit = here[:, None] == jnp.arange(exp_dev, dtype=jnp.int32)[None, :, None, None]
    scale = jnp.sum(jnp.where(hit, meta[:, None, :top], 0.0), 2)
    chosen = jnp.any(hit, 2)
    before = jnp.triu(jnp.ones((tok, tok), BF16), 1)
    rank = jnp.einsum("set,tu->seu", chosen.astype(BF16), before, preferred_element_type=F32)
    base = (jnp.arange(sources, dtype=jnp.int32) % GROUP * C)[:, None, None]
    place = jnp.where(chosen, base + rank.astype(jnp.int32), -1)

    def by_group(a):
        a = a.reshape(4, inner, GROUP, exp_dev, tok)
        return jnp.swapaxes(a, 2, 3).reshape(4, inner, exp_dev, span)

    place, scale = by_group(place), by_group(scale)
    at = place[:, :, :, None, :] == jnp.arange(rows, dtype=jnp.int32)[:, None]

    sent = jnp.einsum("bgert,bgtd->bgerd", at.astype(BF16), every, preferred_element_type=F32).astype(BF16)
    sent = relative(sent)

    chunks = min(CHUNKS, exp_dev)
    per = exp_dev // chunks
    outs = []
    for i in range(chunks):
        own = slice(i * per, (i + 1) * per)
        picked = sent[:, :, :, own]

        def project(weight):
            def piece(x):
                return jnp.einsum("ygerd,edf->ygerf", x, weight[own], preferred_element_type=F32)

            got = lax.ppermute(piece(picked[:, 1]).astype(BF16), "dp", over_core)
            total = piece(picked[:, 0]) + got.astype(F32)
            got = lax.ppermute(total[1].astype(BF16), "dp", over_far)
            return total[0] + got.astype(F32)

        hidden = (jax.nn.silu(project(gate_weight)) * project(up_weight)).astype(BF16)
        other = lax.ppermute(hidden, "dp", over_far)
        pair = jnp.stack([hidden, other])
        hidden = jnp.stack([pair, jnp.stack([lax.ppermute(hidden, "dp", over_core), lax.ppermute(other, "dp", over_core)])], 1)
        outs.append(jnp.einsum("yxgerf,efd->yxgerd", hidden, down_weight[own], preferred_element_type=F32).astype(BF16))
    out = jnp.concatenate(outs, 3)
    out = relative(out.reshape((4,) + out.shape[2:])).reshape((4,) + out.shape[2:])

    weight = jnp.where(at, scale[:, :, :, None, :], 0.0)
    high = weight.astype(BF16)
    low = (weight - high.astype(F32)).astype(BF16)
    both = jnp.concatenate([high, low], 3)
    out = jnp.concatenate([out, out], 3)
    mixed = jnp.einsum("bgert,bgerd->bgtd", both, out, preferred_element_type=F32).astype(BF16)
    mixed = mixed.reshape(n_ep * n_dp * tok, part_d)
    mixed = lax.psum_scatter(mixed, "ep", scatter_dimension=0, tiled=True)
    mixed = lax.all_to_all(mixed, "dp", split_axis=0, concat_axis=1, tiled=True)
    return mixed.astype(BF16)


def solution(mesh):
    in_specs = (
        P(("dp", "ep"), None),
        P(("dp", "ep"), None),
        P(("dp", "ep"), None),
        P(),
        P("ep", "dp", None),
        P("ep", "dp", None),
        P("ep", None, "dp"),
    )
    out_specs = P(("dp", "ep"), None)
    return jax.shard_map(local, mesh=mesh, in_specs=in_specs, out_specs=out_specs, check_vma=False)
```

```python
import jax
import jax.numpy as jnp
from jax import lax
from jax.sharding import PartitionSpec as P

C = 13
CHUNKS = 4
F32 = jnp.float32
BF16 = jnp.bfloat16


def local(tokens, expert_ids, gate_scales, expert_slot, gate_weight, up_weight, down_weight):
    tok = tokens.shape[0]
    top = expert_ids.shape[1]
    experts = expert_slot.shape[0]
    exp_dev, part_d, ff = gate_weight.shape
    n_dp = lax.axis_size("dp")
    n_ep = lax.axis_size("ep")
    chunks = min(CHUNKS, exp_dev)
    per = exp_dev // chunks
    room = n_dp * C
    chunk_rows = n_ep * per * room
    me_dp = lax.axis_index("dp")
    core, far = me_dp % 2, me_dp // 2
    over_core = [(i, i ^ 1) for i in range(4)]
    over_far = [(i, i ^ 2) for i in range(4)]

    def relative(a):
        a = a.reshape((2, 2) + a.shape[1:])
        a = jnp.where(core == 0, a, jnp.concatenate([a[:, 1:], a[:, :1]], 1))
        return jnp.where(far == 0, a, jnp.concatenate([a[1:], a[:1]], 0))

    mine = lax.all_to_all(tokens, "dp", split_axis=1, concat_axis=0, tiled=True)
    same = expert_ids[:, :, None] == jnp.arange(experts, dtype=jnp.int32)
    slot = jnp.sum(jnp.where(same, expert_slot, 0), 2)
    meta = jnp.concatenate([gate_scales, slot.astype(F32)], 1).T
    meta = lax.all_gather(meta, "dp", axis=0)
    slot = meta[:, top:].astype(jnp.int32)
    hit = slot[:, None] == jnp.arange(experts, dtype=jnp.int32)[None, :, None, None]
    chosen = jnp.any(hit, 2).astype(BF16)
    before = jnp.triu(jnp.ones((tok, tok), BF16), 1)
    rank = jnp.einsum("set,tu->seu", chosen, before, preferred_element_type=F32).astype(jnp.int32)
    rank = jnp.sum(jnp.where(hit, rank[:, :, None], 0), 1)
    ep, at = slot // exp_dev, slot % exp_dev
    row = ((at // per * n_ep + ep) * per + at % per) * room
    row = row + jnp.arange(n_dp, dtype=jnp.int32)[:, None, None] * C + rank
    row = jnp.swapaxes(row, 0, 1).reshape(top, n_dp * tok)
    scale = jnp.swapaxes(meta[:, :top], 0, 1).reshape(top, n_dp * tok)

    def places(i):
        rows = i * chunk_rows + jnp.arange(chunk_rows, dtype=jnp.int32)
        return [rows[:, None] == row[k] for k in range(top)]

    total = jnp.zeros((n_dp * tok, part_d), F32)
    for i in range(chunks):
        own = slice(i * per, (i + 1) * per)
        which = sum(p.astype(F32) for p in places(i)).astype(BF16)
        sent = jnp.dot(which, mine, preferred_element_type=F32).astype(BF16)
        x = lax.all_to_all(sent, "ep", split_axis=0, concat_axis=0, tiled=True)
        x = jnp.swapaxes(x.reshape(4, n_ep // 4, per, room, part_d), 1, 2)
        x = relative(x.reshape(4, per, n_ep // 4 * room, part_d))

        def project(weight):
            def piece(x):
                return jnp.einsum("yerd,edf->yerf", x, weight[own], preferred_element_type=F32)

            got = lax.ppermute(piece(x[:, 1]), "dp", over_core)
            both = piece(x[:, 0]) + got
            got = lax.ppermute(both[1].astype(BF16), "dp", over_far)
            return both[0] + got.astype(F32)

        hidden = (jax.nn.silu(project(gate_weight)) * project(up_weight)).astype(BF16)
        other = lax.ppermute(hidden, "dp", over_far)
        pair = jnp.stack([hidden, other])
        hidden = jnp.stack([pair, jnp.stack([lax.ppermute(hidden, "dp", over_core), lax.ppermute(other, "dp", over_core)])], 1)
        out = jnp.einsum("yxerf,efd->yxerd", hidden, down_weight[own], preferred_element_type=F32).astype(BF16)
        out = relative(out.reshape((4,) + out.shape[2:])).reshape(4, per, n_ep // 4, room, part_d)
        out = jnp.swapaxes(out, 1, 2).reshape(chunk_rows, part_d)
        out = lax.all_to_all(out, "ep", split_axis=0, concat_axis=0, tiled=True)

        weight = sum(jnp.where(p, scale[k], 0.0) for k, p in enumerate(places(i)))
        high = weight.astype(BF16)
        low = (weight - high.astype(F32)).astype(BF16)
        weight = jnp.concatenate([high, low], 0)
        total = total + jnp.einsum("rt,rd->td", weight, jnp.concatenate([out, out], 0), preferred_element_type=F32)

    return lax.all_to_all(total.astype(BF16), "dp", split_axis=0, concat_axis=1, tiled=True)


def solution(mesh):
    in_specs = (
        P(("dp", "ep"), None),
        P(("dp", "ep"), None),
        P(("dp", "ep"), None),
        P(),
        P("ep", "dp", None),
        P("ep", "dp", None),
        P("ep", None, "dp"),
    )
    out_specs = P(("dp", "ep"), None)
    return jax.shard_map(local, mesh=mesh, in_specs=in_specs, out_specs=out_specs, check_vma=False)
```

```python
import jax
import jax.numpy as jnp
from jax import lax
from jax.sharding import PartitionSpec as P

C = 13
CHUNKS = 4
F32 = jnp.float32
BF16 = jnp.bfloat16


def local(tokens, expert_ids, gate_scales, expert_slot, gate_weight, up_weight, down_weight):
    tok = tokens.shape[0]
    top = expert_ids.shape[1]
    experts = expert_slot.shape[0]
    exp_dev, part_d, ff = gate_weight.shape
    n_dp = lax.axis_size("dp")
    n_ep = lax.axis_size("ep")
    chunks = min(CHUNKS, exp_dev)
    per = exp_dev // chunks
    room = n_dp * C
    chunk_rows = n_ep * per * room
    me_dp = lax.axis_index("dp")
    core, far = me_dp % 2, me_dp // 2
    over_core = [(i, i ^ 1) for i in range(4)]
    over_far = [(i, i ^ 2) for i in range(4)]

    def relative(a):
        a = a.reshape((2, 2) + a.shape[1:])
        a = jnp.where(core == 0, a, jnp.concatenate([a[:, 1:], a[:, :1]], 1))
        return jnp.where(far == 0, a, jnp.concatenate([a[1:], a[:1]], 0))

    mine = lax.all_to_all(tokens, "dp", split_axis=1, concat_axis=0, tiled=True)
    same = expert_ids[:, :, None] == jnp.arange(experts, dtype=jnp.int32)
    slot = jnp.sum(jnp.where(same, expert_slot, 0), 2)
    meta = jnp.concatenate([gate_scales, slot.astype(F32)], 1).T
    meta = lax.all_gather(meta, "dp", axis=0)
    slot = meta[:, top:].astype(jnp.int32)
    hit = slot[:, None] == jnp.arange(experts, dtype=jnp.int32)[None, :, None, None]
    chosen = jnp.any(hit, 2).astype(BF16)
    before = jnp.triu(jnp.ones((tok, tok), BF16), 1)
    rank = jnp.einsum("set,tu->seu", chosen, before, preferred_element_type=F32).astype(jnp.int32)
    rank = jnp.sum(jnp.where(hit, rank[:, :, None], 0), 1)
    ep, at = slot // exp_dev, slot % exp_dev
    row = ((at // per * n_ep + ep) * per + at % per) * room
    row = row + jnp.arange(n_dp, dtype=jnp.int32)[:, None, None] * C + rank
    row = jnp.swapaxes(row, 0, 1).reshape(top, n_dp * tok)
    scale = jnp.swapaxes(meta[:, :top], 0, 1).reshape(top, n_dp * tok)

    def places(i):
        rows = i * chunk_rows + jnp.arange(chunk_rows, dtype=jnp.int32)
        return [rows[:, None] == row[k] for k in range(top)]

    def tie(*arrays):
        return lax.optimization_barrier(arrays)

    def dispatch(i):
        which = sum(p.astype(F32) for p in places(i)).astype(BF16)
        return jnp.dot(which, mine, preferred_element_type=F32).astype(BF16)

    def exchange(rows):
        return lax.all_to_all(rows, "ep", split_axis=0, concat_axis=0, tiled=True)

    def arrange(x):
        x = jnp.swapaxes(x.reshape(4, n_ep // 4, per, room, part_d), 1, 2)
        return relative(x.reshape(4, per, n_ep // 4 * room, part_d))

    def part(i, x, weight):
        w = weight[i * per:(i + 1) * per]
        return jnp.einsum("yerd,edf->yerf", x, w, preferred_element_type=F32)

    def down(i, hidden, other):
        pair = jnp.stack([hidden, other])
        rest = jnp.stack([lax.ppermute(hidden, "dp", over_core), lax.ppermute(other, "dp", over_core)])
        hidden = jnp.stack([pair, rest], 1)
        w = down_weight[i * per:(i + 1) * per]
        out = jnp.einsum("yxerf,efd->yxerd", hidden, w, preferred_element_type=F32).astype(BF16)
        out = relative(out.reshape((4,) + out.shape[2:])).reshape(4, per, n_ep // 4, room, part_d)
        return jnp.swapaxes(out, 1, 2).reshape(chunk_rows, part_d)

    def combine(i, out):
        weight = sum(jnp.where(p, scale[k], 0.0) for k, p in enumerate(places(i)))
        high = weight.astype(BF16)
        low = (weight - high.astype(F32)).astype(BF16)
        weight = jnp.concatenate([high, low], 0)
        return jnp.einsum("rt,rd->td", weight, jnp.concatenate([out, out], 0), preferred_element_type=F32)

    x = {0: exchange(dispatch(0))}
    kept, far_sent, far_got, hidden, other, out, back = {}, {}, {}, {}, {}, {}, {}

    def finish(i):
        gate, up = (k + g.astype(F32) for k, g in zip(kept[i], far_got[i]))
        hidden[i] = (jax.nn.silu(gate) * up).astype(BF16)

    def send_hidden(i):
        other[i] = lax.ppermute(hidden[i], "dp", over_far)

    def send_out(i):
        out[i] = down(i, hidden[i], other[i])

    for i in range(chunks):
        rows = arrange(x[i]) if i == 0 else x[i]
        if i >= 2:
            finish(i - 2)
            hidden[i - 2], rows = tie(hidden[i - 2], rows)
            send_hidden(i - 2)
        if i >= 1:
            rows, *far_sent[i - 1] = tie(rows, *far_sent[i - 1])
            far_got[i - 1] = [lax.ppermute(a, "dp", over_far) for a in far_sent[i - 1]]
            rows = arrange(rows)
        if i + 1 < chunks:
            sent, rows = tie(dispatch(i + 1), rows)
            x[i + 1] = exchange(sent)
        core_got = [lax.ppermute(part(i, rows[:, 1], w), "dp", over_core) for w in (gate_weight, up_weight)]
        both = [part(i, rows[:, 0], w) + g for w, g in zip((gate_weight, up_weight), core_got)]
        kept[i] = [b[0] for b in both]
        far_sent[i] = [b[1].astype(BF16) for b in both]
        if i >= 3:
            send_out(i - 3)
            out[i - 3], *far_sent[i] = tie(out[i - 3], *far_sent[i])
            back[i - 3] = exchange(out[i - 3])
    last = chunks - 1
    far_got[last] = [lax.ppermute(a, "dp", over_far) for a in far_sent[last]]
    for i in range(chunks):
        if i not in hidden:
            finish(i)
            if i >= 2:
                if i - 2 not in back:
                    out[i - 2], hidden[i] = tie(out[i - 2], hidden[i])
                    back[i - 2] = exchange(out[i - 2])
                if i >= 3:
                    back[i - 3], hidden[i] = tie(back[i - 3], hidden[i])
            send_hidden(i)
        if i not in out:
            send_out(i)
    total = jnp.zeros((n_dp * tok, part_d), F32)
    for i in range(chunks):
        if i not in back:
            back[i] = exchange(out[i])
        total = total + combine(i, back[i])
    return lax.all_to_all(total.astype(BF16), "dp", split_axis=0, concat_axis=1, tiled=True)


def solution(mesh):
    in_specs = (
        P(("dp", "ep"), None),
        P(("dp", "ep"), None),
        P(("dp", "ep"), None),
        P(),
        P("ep", "dp", None),
        P("ep", "dp", None),
        P("ep", None, "dp"),
    )
    out_specs = P(("dp", "ep"), None)
    return jax.shard_map(local, mesh=mesh, in_specs=in_specs, out_specs=out_specs, check_vma=False)
```
